256 devices in a mesh: gx: 64 (over y, z, core), gy: 4 (over x).
Axes of the slice: x: 4, y: 4, z: 8, core: 2. Of those that a mesh axis runs over, the one named last changes fastest.
Arguments:
- coupling: float32 [1024, 64, 64], P('gx'), may hold values from -20 to 1920, as said below
- vertical: float32 [1024, 64, 64], P('gx'), may hold values from -10 to 21, as said below
- source: float32 [1024, 512, 64], P('gx', 'gy'), may hold values from -60 to 60
- previous: float32 [1024, 512, 64], P('gx', 'gy'), may hold values from -24 to 24
- spread_rate: float32 [64], replicated, may hold values from 0.5 to 2
Outputs:
- updated: float32 [1024, 512, 64], P('gx', 'gy')
The draws below stay inside these ranges and needn't reach their ends.
Inputs may be any that keep to these rules, and one draw needn't show every extreme that they name: `coupling`: each block is symmetric positive definite. `vertical`: each block is symmetric, tridiagonal and positive definite.
All inputs are finite; a program needn't handle non-finite values.
Results may differ from the reference program's by a relative error of at most 0.0015.
Values sent between devices are 32-bit elements; how exact they have to be, the bound alone decides.
A program may use at most 192 MiB of HBM per device.

```python
import math
import jax
import jax.numpy as jnp
from jax import lax

LEVELS = 64
NX = 1024
NY = 512


def draw_coupling(key, part):
    key = jax.random.fold_in(key, 11)
    key_rate, key_diag, key_noise = jax.random.split(key, 3)
    rate = jnp.exp(jax.random.uniform(key_rate, (NX, 1, 1), jnp.float32, math.log(5.0), math.log(20.0)))
    diag_part = LEVELS + 0.5 * LEVELS * jax.random.uniform(key_diag, (NX, LEVELS, 1), jnp.float32)
    noise = jax.random.uniform(key_noise, (NX, LEVELS, LEVELS), jnp.float32, -1.0, 1.0)
    identity = jnp.eye(LEVELS, dtype=jnp.float32)
    offdiag = 0.5 * (noise + jnp.swapaxes(noise, 1, 2)) * (1.0 - identity)
    return (rate * (identity * diag_part + offdiag)).astype(jnp.float32)


def draw_vertical(key, part):
    key = jax.random.fold_in(key, 23)
    key_time, key_diff = jax.random.split(key, 2)
    base = 1200.0 * LEVELS / (NX * NX)
    timescale = base * jnp.exp(jax.random.uniform(key_time, (NX, 1), jnp.float32, math.log(0.5), math.log(2.0)))
    interface = jnp.exp(jax.random.uniform(key_diff, (NX, LEVELS), jnp.float32, 0.0, math.log(10.0)))
    level_index = jnp.arange(LEVELS)
    interface = interface * (level_index < LEVELS - 1)[None, :]
    below = jnp.concatenate([jnp.zeros((NX, 1), jnp.float32), interface[:, :-1]], axis=1)
    diagonal = timescale + interface + below
    row_index = level_index[:, None]
    col_index = level_index[None, :]
    identity = (row_index == col_index).astype(jnp.float32)
    upper_mask = (col_index == row_index + 1).astype(jnp.float32)
    lower_mask = (row_index == col_index + 1).astype(jnp.float32)
    block = identity * diagonal[:, :, None] - upper_mask * interface[:, :, None] - lower_mask * interface[:, None, :]
    return block.astype(jnp.float32)


def draw_source(key, part):
    key = jax.random.fold_in(key, 37)
    rough = jnp.clip(jax.random.normal(key, (NX, NY, LEVELS), jnp.float32), -6.0, 6.0)
    return (10.0 * rough).astype(jnp.float32)


def block_scale(stream_key, shape, shards, smallest, largest):
    gain, own = 1.0, jax.random.fold_in(stream_key, 6)
    for axis_at, shards_of in shards:
        steps = jnp.exp(jax.random.uniform(jax.random.fold_in(own, axis_at), (shards_of,), jnp.float32, smallest / len(shards), largest / len(shards)))
        gain = gain * jnp.repeat(steps, shape[axis_at] // shards_of).reshape([-1 if axis == axis_at else 1 for axis in range(len(shape))])
    return gain


def bell_draw(stream_key, shape, deviation, bound, shards=(), held_as=jnp.bfloat16):
    array = jax.random.normal(stream_key, shape, jnp.float32) * deviation
    if len(shards) > 0:
        array = block_scale(stream_key, shape, shards, -0.22, 0.18) * array
    return jnp.clip(array, min=-bound, max=bound).astype(held_as)


def setup_inputs(seed: int = 0) -> dict:
    seeds = jax.random.split(jax.random.key(seed), 6)
    return {
        "coupling": draw_coupling(jax.random.fold_in(seeds[5], 71), 0),
        "vertical": draw_vertical(jax.random.fold_in(seeds[5], 71), 0),
        "source": draw_source(jax.random.fold_in(seeds[5], 71), 0),
        "previous": bell_draw(seeds[3], (NX, NY, LEVELS), 4.0, 24.0, ((0, 64), (1, 4)), jnp.float32),
        "spread_rate": jnp.clip(jnp.exp(jax.random.uniform(seeds[4], (LEVELS,), jnp.float32, math.log(0.5), math.log(2.0))), 0.5, 2.0),
    }


def product(left, right):
    return jnp.matmul(left, right, precision=lax.Precision.HIGHEST)

def forward_step(running, items):
    block, link, right = items
    factor = jnp.linalg.cholesky(block - running[0])
    spread = jax.scipy.linalg.cho_solve((factor, True), link)
    partial_sol = jax.scipy.linalg.cho_solve((factor, True), right + running[1])
    return ((product(link, spread), product(link, partial_sol)), (spread, partial_sol))

def backward_step(running, items):
    spread, partial_sol = items
    value = partial_sol + product(spread, running)
    return (value, value)

def reference(coupling, vertical, source, previous, spread_rate):
    forcing = source + spread_rate * (jnp.roll(previous, -1, axis=1) + jnp.roll(previous, 1, axis=1) - 2.0 * previous)
    prior = jnp.concatenate([jnp.zeros_like(coupling[:1]), coupling[:-1]], axis=0)
    blocks = vertical + prior + coupling
    columns = jnp.swapaxes(forcing, 1, 2)
    width = coupling.shape[1]
    start = (jnp.zeros((width, width), jnp.float32), jnp.zeros_like(columns[0]))
    _, (spreads, partials) = lax.scan(forward_step, start, (blocks, coupling, columns))
    _, solved = lax.scan(backward_step, jnp.zeros_like(columns[0]), (spreads, partials), reverse=True)
    return jnp.swapaxes(solved, 1, 2)
```

```python
import jax
import jax.numpy as jnp
from jax import lax
from jax.experimental import pallas as pl
from jax.experimental.pallas import tpu as pltpu
from jax.sharding import PartitionSpec as P

CELLS = 16
ROWS = 128
W = 64
CHIPS_Z = 8
CHIPS_Y = 4
CHIPS_X = 4
MESH = pl.DeviceIdType.MESH


def dot(left, right, left_dim=1):
    return lax.dot_general(
        left,
        right,
        (((left_dim,), (0,)), ((), ())),
        precision=lax.Precision.HIGHEST,
        preferred_element_type=jnp.float32,
    )


def iota(shape, dim):
    return lax.broadcasted_iota(jnp.int32, shape, dim)


def lane_copy(value, lane):
    return jnp.broadcast_to(lax.slice_in_dim(value, lane, lane + 1, axis=2), value.shape)


def inverse(augmented):
    sub = iota((1, 8, 128), 1)

    def block(_, value):
        columns = [lane_copy(value, j) for j in range(8)]
        turned = pltpu.roll(value, 120, 2)
        top = turned[:, :8]
        head = [column[:, :8] for column in columns]
        recip = 1.0 / head[0][:, 0:1]
        for j in range(8):
            next_recip = None
            if j < 7:
                cross = head[j][:, j + 1 : j + 2] * head[j + 1][:, j : j + 1]
                next_recip = 1.0 / (head[j + 1][:, j + 1 : j + 2] - cross * recip)
            row = top[:, j : j + 1] * recip
            for k in range(j + 1, 8):
                entry = head[k][:, j : j + 1] * recip
                head[k] = jnp.where(sub == j, entry, head[k] - head[j] * entry)
            top = jnp.where(sub == j, row, top - head[j] * row)
            recip = next_recip
        terms = [columns[j][:, 8:] * top[:, j : j + 1] for j in range(8)]
        total = ((terms[0] + terms[1]) + (terms[2] + terms[3])) + (
            (terms[4] + terms[5]) + (terms[6] + terms[7])
        )
        return jnp.concatenate([turned[:, 8:] - total, top], axis=1)

    return lax.fori_loop(0, 8, block, augmented)


def augmented(link_excess, left):
    lane = iota((W, 128), 1)
    eye = (lane == iota((W, 128), 0) + W).astype(jnp.float32)
    value = link_excess + pltpu.roll(link_excess, W, 1)
    if left is not None:
        value = value + jnp.concatenate([left, left], axis=0).T[:W]
    return jnp.where(lane < W, value, eye)


def reduce_nodes(nodes, ghost, solved, count):
    lane = iota((W, 128), 1)
    stride = 1
    while stride < count:
        picks = range(stride, count, 2 * stride)
        inverses = inverse(
            jnp.stack([augmented(nodes[i, 0], nodes[i - stride, 0]) for i in picks])
        )
        for at, i in enumerate(picks):
            both = jnp.concatenate([nodes[i, 0], nodes[i, 1]], axis=1)
            answer = dot(inverses[at][:, :W], both)
            solved[i, 0] = answer[:, :128]
            solved[i, 1] = answer[:, 128:]
            before = nodes[i - stride, 0]
            to_left = dot(before[:, :W], answer)
            nodes[i - stride, 0] = jnp.where(lane < W, 0.0, before) + to_left[:, :128]
            nodes[i - stride, 1] = nodes[i - stride, 1] + to_left[:, 128:]
            to_right = dot(nodes[i, 0][:, :W], answer, 0)
            excess = jnp.where(lane < W, 0.0, to_right[:, :128])
            if i + stride < count:
                nodes[i + stride, 0] = nodes[i + stride, 0] + excess
                nodes[i + stride, 1] = nodes[i + stride, 1] + to_right[:, 128:]
            elif ghost is not None:
                ghost[0] = ghost[0] + excess
                ghost[1] = ghost[1] + to_right[:, 128:]
        stride *= 2


def expand_nodes(solved, field, count):
    stride = count // 2
    while stride >= 1:
        for i in range(stride, count, 2 * stride):
            before, after = field[i - stride], field[i + stride]
            change = jnp.concatenate([after - before, -before], axis=0)
            field[i] = solved[i, 1] + before + dot(solved[i, 0], change)
        stride //= 2


def chain(slots, nodes, ghost, count):
    lane = iota((W, 128), 1)
    for i in range(count):
        if i == 0:
            nodes[0] = slots[0, 0:2]
        else:
            nodes[i, 0] = slots[i, 0] + jnp.where(lane < W, 0.0, slots[i - 1, 2])
            nodes[i, 1] = slots[i, 1] + slots[i - 1, 3]
    if ghost is not None:
        ghost[...] = slots[count - 1, 2:4]


def kernel(
    coupling,
    vertical,
    source,
    previous,
    rate,
    out,
    edge_out,
    edge_in,
    nodes,
    ghost,
    solved,
    field,
    pair_slots,
    pair_nodes,
    pair_ghost,
    pair_solved,
    pair_field,
    z_slots,
    z_nodes,
    z_ghost,
    z_solved,
    z_field,
    y_slots,
    y_nodes,
    y_solved,
    y_field,
    edge_send,
    edge_recv,
    pair_send,
    pair_recv,
    z_send,
    z_recv,
    y_send,
    y_recv,
):
    gx, gy = lax.axis_index("gx"), lax.axis_index("gy")
    core = lax.rem(gx, 2)
    chip = lax.div(gx, 2)
    z = lax.rem(chip, CHIPS_Z)
    y = lax.div(chip, CHIPS_Z)

    def at(y_, z_, core_):
        return (y_ * CHIPS_Z + z_) * 2 + core_

    x_up = (gx, lax.rem(gy + 1, CHIPS_X))
    x_down = (gx, lax.rem(gy + CHIPS_X - 1, CHIPS_X))
    partner = (at(y, z, 1 - core), gy)
    z_to = [(at(y, lax.rem(z + d, CHIPS_Z), core), gy) for d in range(1, CHIPS_Z)]
    y_to = [(at(lax.rem(y + d, CHIPS_Y), z, core), gy) for d in range(1, CHIPS_Y)]

    barrier = pltpu.get_barrier_semaphore()
    everyone = [x_up, x_down, partner] + z_to + y_to
    for peer in everyone:
        pl.semaphore_signal(barrier, inc=1, device_id=peer, device_id_type=MESH)
    edge_out[...] = jnp.zeros_like(edge_out)
    edge_out[0, :, 0:W] = previous[:, ROWS - 1, :]
    edge_out[1, :, 0:W] = previous[:, 0, :]
    pl.semaphore_wait(barrier, len(everyone))

    def remote(src, dst, send, recv, peer):
        copy = pltpu.make_async_remote_copy(
            src_ref=src,
            dst_ref=dst,
            send_sem=send,
            recv_sem=recv,
            device_id=peer,
            device_id_type=MESH,
        )
        copy.start()
        return copy

    edges = [
        remote(edge_out.at[0], edge_in.at[0], edge_send.at[0], edge_recv.at[0], x_up),
        remote(edge_out.at[1], edge_in.at[1], edge_send.at[1], edge_recv.at[1], x_down),
    ]

    lane = iota((W, 128), 1)
    for i in range(CELLS):
        nodes[i, 0, :, 0:W] = coupling[i]
        nodes[i, 0, :, W:128] = vertical[i]
    for edge in edges:
        edge.wait()
    row_index = iota((ROWS, W), 0)
    for i in range(CELLS):
        own = previous[i]
        below = jnp.where(row_index == 0, edge_in[0, i : i + 1, 0:W], pltpu.roll(own, 1, 0))
        above = jnp.where(
            row_index == ROWS - 1, edge_in[1, i : i + 1, 0:W], pltpu.roll(own, ROWS - 1, 0)
        )
        forcing = source[i] + rate[...] * (above + below - 2.0 * own)
        nodes[i, 1] = forcing.T
    ghost[...] = jnp.zeros_like(ghost)
    reduce_nodes(nodes, ghost, solved, CELLS)

    pair_slots[core, 0:2] = nodes[0]
    pair_slots[core, 2:4] = ghost[...]
    remote(
        pair_slots.at[core], pair_slots.at[core], pair_send.at[0], pair_recv.at[0], partner
    ).wait()
    chain(pair_slots, pair_nodes, pair_ghost, 2)
    reduce_nodes(pair_nodes, pair_ghost, pair_solved, 2)

    z_slots[z, 0:2] = pair_nodes[0]
    z_slots[z, 2:4] = pair_ghost[...]
    sends = [
        remote(z_slots.at[z], z_slots.at[z], z_send.at[d], z_recv.at[d], z_to[d])
        for d in range(CHIPS_Z - 1)
    ]
    for send in sends:
        send.wait()
    chain(z_slots, z_nodes, z_ghost, CHIPS_Z)
    reduce_nodes(z_nodes, z_ghost, z_solved, CHIPS_Z)

    y_slots[y, 0:2] = z_nodes[0]
    y_slots[y, 2:4] = z_ghost[...]
    sends = [
        remote(y_slots.at[y], y_slots.at[y], y_send.at[d], y_recv.at[d], y_to[d])
        for d in range(CHIPS_Y - 1)
    ]
    for send in sends:
        send.wait()
    chain(y_slots, y_nodes, None, CHIPS_Y)
    reduce_nodes(y_nodes, None, y_solved, CHIPS_Y)

    first = inverse(augmented(y_nodes[0, 0], None)[None])
    y_field[0] = dot(first[0][:, :W], y_nodes[0, 1])
    y_field[CHIPS_Y] = jnp.zeros((W, ROWS), jnp.float32)
    expand_nodes(y_solved, y_field, CHIPS_Y)
    z_field[0] = y_field[y]
    z_field[CHIPS_Z] = y_field[y + 1]
    expand_nodes(z_solved, z_field, CHIPS_Z)
    pair_field[0] = z_field[z]
    pair_field[2] = z_field[z + 1]
    expand_nodes(pair_solved, pair_field, 2)
    field[0] = pair_field[core]
    field[CELLS] = pair_field[core + 1]
    expand_nodes(solved, field, CELLS)
    for i in range(CELLS):
        out[i] = field[i].T


def local(coupling, vertical, source, previous, spread_rate):
    f32 = jnp.float32

    def vmem(*shape):
        return pltpu.VMEM(shape + (W, 128), f32)

    dma = pltpu.SemaphoreType.DMA
    return pl.pallas_call(
        kernel,
        out_shape=jax.ShapeDtypeStruct((CELLS, ROWS, W), f32),
        in_specs=[pl.BlockSpec(memory_space=pltpu.VMEM)] * 5,
        out_specs=pl.BlockSpec(memory_space=pltpu.VMEM),
        scratch_shapes=[
            pltpu.VMEM((2, CELLS, 128), f32),
            pltpu.VMEM((2, CELLS, 128), f32),
            vmem(CELLS, 2),
            vmem(2),
            vmem(CELLS, 2),
            vmem(CELLS + 1),
            vmem(2, 4),
            vmem(2, 2),
            vmem(2),
            vmem(2, 2),
            vmem(3),
            vmem(CHIPS_Z, 4),
            vmem(CHIPS_Z, 2),
            vmem(2),
            vmem(CHIPS_Z, 2),
            vmem(CHIPS_Z + 1),
            vmem(CHIPS_Y, 4),
            vmem(CHIPS_Y, 2),
            vmem(CHIPS_Y, 2),
            vmem(CHIPS_Y + 1),
            dma((2,)),
            dma((2,)),
            dma((1,)),
            dma((1,)),
            dma((CHIPS_Z - 1,)),
            dma((CHIPS_Z - 1,)),
            dma((CHIPS_Y - 1,)),
            dma((CHIPS_Y - 1,)),
        ],
        compiler_params=pltpu.CompilerParams(
            collective_id=0, has_side_effects=True, vmem_limit_bytes=48 * 1024 * 1024
        ),
        cost_estimate=pl.CostEstimate(
            flops=400_000_000, bytes_accessed=4_000_000, transcendentals=0
        ),
    )(coupling, vertical, source, previous, spread_rate.reshape(1, W))


def solution(mesh):
    cells = P("gx", None, None)
    slab = P("gx", "gy", None)
    return jax.shard_map(
        local,
        mesh=mesh,
        in_specs=(cells, cells, slab, slab, P()),
        out_specs=slab,
        check_vma=False,
    )
```

```python
import jax
import jax.numpy as jnp
from jax import lax
from jax.experimental import pallas as pl
from jax.experimental.pallas import tpu as pltpu
from jax.sharding import PartitionSpec as P

CELLS = 16
ROWS = 128
W = 64
CHIPS_Z = 8
CHIPS_Y = 4
CHIPS_X = 4
MESH = pl.DeviceIdType.MESH


def dot(left, right, left_dim=1):
    return lax.dot_general(
        left,
        right,
        (((left_dim,), (0,)), ((), ())),
        precision=lax.Precision.HIGH,
        preferred_element_type=jnp.float32,
    )


def iota(shape, dim):
    return lax.broadcasted_iota(jnp.int32, shape, dim)


def lane_copy(value, lane):
    return jnp.broadcast_to(lax.slice_in_dim(value, lane, lane + 1, axis=2), value.shape)


def inverse(augmented):
    sub = iota((1, 8, 128), 1)

    def block(_, value):
        columns = [lane_copy(value, j) for j in range(8)]
        turned = pltpu.roll(value, 120, 2)
        top = turned[:, :8]
        head = [column[:, :8] for column in columns]
        recip = 1.0 / head[0][:, 0:1]
        for j in range(8):
            next_recip = None
            if j < 7:
                cross = head[j][:, j + 1 : j + 2] * head[j + 1][:, j : j + 1]
                next_recip = 1.0 / (head[j + 1][:, j + 1 : j + 2] - cross * recip)
            row = top[:, j : j + 1] * recip
            for k in range(j + 1, 8):
                entry = head[k][:, j : j + 1] * recip
                head[k] = jnp.where(sub == j, entry, head[k] - head[j] * entry)
            top = jnp.where(sub == j, row, top - head[j] * row)
            recip = next_recip
        terms = [columns[j][:, 8:] * top[:, j : j + 1] for j in range(8)]
        total = ((terms[0] + terms[1]) + (terms[2] + terms[3])) + (
            (terms[4] + terms[5]) + (terms[6] + terms[7])
        )
        return jnp.concatenate([turned[:, 8:] - total, top], axis=1)

    return lax.fori_loop(0, 8, block, augmented)


def augmented(link_excess, left, symmetric=False):
    lane = iota((W, 128), 1)
    eye = (lane == iota((W, 128), 0) + W).astype(jnp.float32)
    value = link_excess + pltpu.roll(link_excess, W, 1)
    if left is not None:
        value = value + (left if symmetric else jnp.concatenate([left, left], axis=0).T[:W])
    return jnp.where(lane < W, value, eye)


def high_lanes(value):
    return jnp.where(iota(value.shape, 1) < W, 0.0, value)


def picks_of(stride, count):
    return range(stride, count, 2 * stride)


def strides_of(count):
    return [1 << k for k in range(count.bit_length() - 1)]


def reduce_links(links, ghost, solved, inverses, count, stride, symmetric=False):
    picks = picks_of(stride, count)
    found = inverse(
        jnp.stack([augmented(links[i], links[i - stride], symmetric) for i in picks])
    )
    for at, i in enumerate(picks):
        inverses[i] = found[at]
        answer = dot(found[at][:, :W], links[i])
        solved[i] = answer
        before = links[i - stride]
        links[i - stride] = high_lanes(before) + dot(before[:, :W], answer)
        if i + stride < count:
            links[i + stride] = links[i + stride] + high_lanes(dot(links[i][:, :W], answer, 0))
        elif ghost is not None:
            ghost[...] = ghost[...] + high_lanes(dot(links[i][:, :W], answer, 0))


def reduce_rhs(rhs, ghost, solved, inverses, count, stride):
    for i in picks_of(stride, count):
        own = rhs[i]
        passed = dot(solved[i], own, 0)
        rhs[i - stride] = rhs[i - stride] + (own - passed[:W] - passed[W:])
        if i + stride < count:
            rhs[i + stride] = rhs[i + stride] + passed[:W]
        elif ghost is not None:
            ghost[...] = ghost[...] + passed[:W]
        rhs[i] = dot(inverses[i][:, :W], own)


def expand(solved, rhs, field, count):
    for stride in reversed(strides_of(count)):
        for i in picks_of(stride, count):
            before, after = field[i - stride], field[i + stride]
            change = jnp.concatenate([after - before, -before], axis=0)
            field[i] = rhs[i] + before + dot(solved[i], change)


def packed_links(link_excess, ghost):
    low = pltpu.roll(ghost[: W // 2], W, 1)
    return jnp.concatenate([link_excess, low + high_lanes(ghost[W // 2 :])], axis=0)


def unpacked_ghost(packed):
    tail = packed[W:]
    return high_lanes(jnp.concatenate([pltpu.roll(tail, W, 1), tail], axis=0))


def chain_links(packed, links, ghost, count):
    for i in range(count):
        value = packed(i)[:W]
        if i > 0:
            value = value + unpacked_ghost(packed(i - 1))
        links[i] = value
    if ghost is not None:
        ghost[...] = unpacked_ghost(packed(count - 1))


def chain_rhs(own, passed, rhs, ghost, count):
    for i in range(count):
        rhs[i] = own(i) + passed(i - 1) if i > 0 else own(i)
    if ghost is not None:
        ghost[...] = passed(count - 1)


def kernel(coupling, vertical, source, previous, rate, out, *scratch):
    (coupling_in, vertical_in, source_in, previous_in, in_sems) = scratch[:5]
    (edge_out, edge_in, edge_send, edge_recv) = scratch[5:9]
    (links, ghost, solved, inverses, rhs, rhs_ghost, field) = scratch[9:16]
    (p_slots, p_links, p_ghost, p_solved, p_inverses) = scratch[16:21]
    (p_rslots, p_rhs, p_rhs_ghost, p_field, p_send, p_recv) = scratch[21:27]
    (z_slots, z_links, z_ghost, z_solved, z_inverses) = scratch[27:32]
    (z_rslots, z_rhs, z_rhs_ghost, z_field, z_send, z_recv, f_send, f_recv) = scratch[32:40]
    (y_slots, y_links, y_solved, y_inverses) = scratch[40:44]
    (y_rslots, y_rhs, y_field, y_send, y_recv) = scratch[44:49]

    gx, gy = lax.axis_index("gx"), lax.axis_index("gy")
    core = lax.rem(gx, 2)
    chip = lax.div(gx, 2)
    z = lax.rem(chip, CHIPS_Z)
    y = lax.div(chip, CHIPS_Z)

    def at(y_, z_, core_):
        return (y_ * CHIPS_Z + z_) * 2 + core_

    x_up = (gx, lax.rem(gy + 1, CHIPS_X))
    x_down = (gx, lax.rem(gy + CHIPS_X - 1, CHIPS_X))
    partner = (at(y, z, 1 - core), gy)
    z_to = {d: (at(y, lax.rem(z + d, CHIPS_Z), core), gy) for d in range(1, CHIPS_Z)}
    y_to = {d: (at(lax.rem(y + d, CHIPS_Y), z, core), gy) for d in range(1, CHIPS_Y)}
    z_order = (4, 3, 5, 2, 6, 1, 7)
    z_arrive = (1, 7, 2, 6, 3, 5, 4)
    y_order = (2, 1, 3)

    barrier = pltpu.get_barrier_semaphore()
    everyone = [x_up, x_down, partner] + list(z_to.values()) + list(y_to.values())
    for peer in everyone:
        pl.semaphore_signal(barrier, inc=1, device_id=peer, device_id_type=MESH)
    loads = [
        pltpu.make_async_copy(src, dst, in_sems.at[k])
        for k, (src, dst) in enumerate(
            [
                (coupling, coupling_in),
                (vertical, vertical_in),
                (previous, previous_in),
                (source, source_in),
            ]
        )
    ]
    for load in loads:
        load.start()

    def remote(src, dst, send, recv, peer):
        copy = pltpu.make_async_remote_copy(
            src_ref=src,
            dst_ref=dst,
            send_sem=send,
            recv_sem=recv,
            device_id=peer,
            device_id_type=MESH,
        )
        copy.start()
        return copy

    lane = iota((W, 128), 1)
    loads[0].wait()
    loads[1].wait()
    for i in range(CELLS):
        links[i, :, 0:W] = coupling_in[i]
        links[i, :, W:128] = vertical_in[i]
    ghost[...] = jnp.zeros_like(ghost)
    reduce_links(links, ghost, solved, inverses, CELLS, 1, True)

    loads[2].wait()
    edges_value = jnp.zeros((W, 128), jnp.float32)
    for i in range(CELLS):
        own = previous_in[i]
        edges_value = jnp.where(lane == i, pltpu.roll(own, i + 1, 1), edges_value)
        edges_value = jnp.where(lane == W + i, pltpu.roll(own, W + i, 1), edges_value)
    edge_out[...] = edges_value
    pl.semaphore_wait(barrier, len(everyone))
    edges = [
        remote(edge_out, edge_in.at[0], edge_send.at[0], edge_recv.at[0], x_up),
        remote(edge_out, edge_in.at[1], edge_send.at[1], edge_recv.at[1], x_down),
    ]
    for stride in strides_of(CELLS)[1:]:
        reduce_links(links, ghost, solved, inverses, CELLS, stride)

    p_slots[core] = packed_links(links[0], ghost[...])
    p_copy = remote(p_slots.at[core], p_slots.at[core], p_send.at[0], p_recv.at[0], partner)

    loads[3].wait()
    for edge in edges:
        edge.wait()
    speed = jnp.broadcast_to(rate[...], (128, W)).T
    for i in range(CELLS):
        own = previous_in[i]
        below = jnp.where(
            lane == 0, pltpu.roll(edge_in[0], (128 - i) % 128, 1), pltpu.roll(own, 1, 1)
        )
        above = jnp.where(
            lane == 127, pltpu.roll(edge_in[1], 127 - W - i, 1), pltpu.roll(own, 127, 1)
        )
        rhs[i] = source_in[i] + speed * (above + below - 2.0 * own)
    rhs_ghost[...] = jnp.zeros_like(rhs_ghost)

    p_copy.wait()
    chain_links(lambda i: p_slots[i], p_links, p_ghost, 2)
    reduce_links(p_links, p_ghost, p_solved, p_inverses, 2, 1)

    payload = packed_links(p_links[0], p_ghost[...])
    z_slots[0, z] = payload[:48]
    z_slots[1, z] = payload[48:]
    z_copies = {
        d: remote(
            z_slots.at[core, z],
            z_slots.at[core, z],
            z_send.at[0, d - 1],
            z_recv.at[0, d - 1],
            z_to[d],
        )
        for d in z_order
    }

    for stride in strides_of(CELLS):
        reduce_rhs(rhs, rhs_ghost, solved, inverses, CELLS, stride)
    p_rslots[core, 0] = rhs[0]
    p_rslots[core, 1] = rhs_ghost[...]
    p_copy = remote(p_rslots.at[core], p_rslots.at[core], p_send.at[1], p_recv.at[1], partner)
    p_copy.wait()
    chain_rhs(lambda i: p_rslots[i, 0], lambda i: p_rslots[i, 1], p_rhs, p_rhs_ghost, 2)
    reduce_rhs(p_rhs, p_rhs_ghost, p_solved, p_inverses, 2, 1)
    z_rslots[0, z] = p_rhs[0]
    z_rslots[1, z] = p_rhs_ghost[...]

    def forward(slots, copies, which):
        passed = []
        for d in z_arrive:
            copies[d].wait_recv()
            behind = lax.rem(z + CHIPS_Z - d, CHIPS_Z)
            passed.append(
                remote(
                    slots.at[core, behind],
                    slots.at[core, behind],
                    f_send.at[which, d - 1],
                    f_recv.at[which, d - 1],
                    partner,
                )
            )
        return passed

    zr_copies = {
        d: remote(
            z_rslots.at[core, z],
            z_rslots.at[core, z],
            z_send.at[1, d - 1],
            z_recv.at[1, d - 1],
            z_to[d],
        )
        for d in z_order
    }
    for copy in forward(z_slots, z_copies, 0):
        copy.wait()
    chain_links(
        lambda i: jnp.concatenate([z_slots[0, i], z_slots[1, i]], axis=0),
        z_links,
        z_ghost,
        CHIPS_Z,
    )
    for stride in strides_of(CHIPS_Z):
        reduce_links(z_links, z_ghost, z_solved, z_inverses, CHIPS_Z, stride)

    y_slots[y] = packed_links(z_links[0], z_ghost[...])
    y_copies = [
        remote(y_slots.at[y], y_slots.at[y], y_send.at[0, d - 1], y_recv.at[0, d - 1], y_to[d])
        for d in y_order
    ]
    for copy in forward(z_rslots, zr_copies, 1):
        copy.wait()
    chain_rhs(lambda i: z_rslots[0, i], lambda i: z_rslots[1, i], z_rhs, z_rhs_ghost, CHIPS_Z)
    for stride in strides_of(CHIPS_Z):
        reduce_rhs(z_rhs, z_rhs_ghost, z_solved, z_inverses, CHIPS_Z, stride)
    y_rslots[y, 0] = z_rhs[0]
    y_rslots[y, 1] = z_rhs_ghost[...]
    yr_copies = [
        remote(
            y_rslots.at[y], y_rslots.at[y], y_send.at[1, d - 1], y_recv.at[1, d - 1], y_to[d]
        )
        for d in y_order
    ]
    for copy in y_copies:
        copy.wait()
    chain_links(lambda i: y_slots[i], y_links, None, CHIPS_Y)
    for stride in strides_of(CHIPS_Y):
        reduce_links(y_links, None, y_solved, y_inverses, CHIPS_Y, stride)
    first = inverse(augmented(y_links[0], None)[None])

    for copy in yr_copies:
        copy.wait()
    chain_rhs(lambda i: y_rslots[i, 0], lambda i: y_rslots[i, 1], y_rhs, None, CHIPS_Y)
    for stride in strides_of(CHIPS_Y):
        reduce_rhs(y_rhs, None, y_solved, y_inverses, CHIPS_Y, stride)
    y_field[0] = dot(first[0][:, :W], y_rhs[0])
    y_field[CHIPS_Y] = jnp.zeros((W, ROWS), jnp.float32)
    expand(y_solved, y_rhs, y_field, CHIPS_Y)
    z_field[0] = y_field[y]
    z_field[CHIPS_Z] = y_field[y + 1]
    expand(z_solved, z_rhs, z_field, CHIPS_Z)
    p_field[0] = z_field[z]
    p_field[2] = z_field[z + 1]
    expand(p_solved, p_rhs, p_field, 2)
    field[0] = p_field[core]
    field[CELLS] = p_field[core + 1]
    expand(solved, rhs, field, CELLS)
    for i in range(CELLS):
        out[i] = field[i]
    for d in z_order:
        z_copies[d].wait_send()
        zr_copies[d].wait_send()


def local(coupling, vertical, source, previous, spread_rate):
    f32 = jnp.float32

    def vmem(*shape):
        return pltpu.VMEM(shape + (128,), f32)

    dma = pltpu.SemaphoreType.DMA

    def level(count):
        return [vmem(count, W), vmem(W), vmem(count, W), vmem(count, W)]

    def level_rhs(count):
        return [vmem(count, W), vmem(W), vmem(count + 1, W)]

    scratch = [
        pltpu.VMEM((CELLS, W, W), f32),
        pltpu.VMEM((CELLS, W, W), f32),
        vmem(CELLS, W),
        vmem(CELLS, W),
        dma((4,)),
        vmem(W),
        vmem(2, W),
        dma((2,)),
        dma((2,)),
    ]
    scratch += level(CELLS) + level_rhs(CELLS)
    scratch += [vmem(2, 96)] + level(2)
    scratch += [vmem(2, 2, W)] + level_rhs(2) + [dma((2,)), dma((2,))]
    scratch += [vmem(2, CHIPS_Z, 48)] + level(CHIPS_Z)
    scratch += [vmem(2, CHIPS_Z, W)] + level_rhs(CHIPS_Z) + [dma((2, CHIPS_Z - 1))] * 4
    scratch += [vmem(CHIPS_Y, 96), vmem(CHIPS_Y, W), vmem(CHIPS_Y, W), vmem(CHIPS_Y, W)]
    scratch += [vmem(CHIPS_Y, 2, W), vmem(CHIPS_Y, W), vmem(CHIPS_Y + 1, W)]
    scratch += [dma((2, CHIPS_Y - 1))] * 2
    anywhere = pl.BlockSpec(memory_space=pl.ANY)
    solved = pl.pallas_call(
        kernel,
        out_shape=jax.ShapeDtypeStruct((CELLS, W, ROWS), f32),
        in_specs=[anywhere] * 4 + [pl.BlockSpec(memory_space=pltpu.VMEM)],
        out_specs=pl.BlockSpec(memory_space=pltpu.VMEM),
        scratch_shapes=scratch,
        compiler_params=pltpu.CompilerParams(
            collective_id=0, has_side_effects=True, vmem_limit_bytes=60 * 1024 * 1024
        ),
        cost_estimate=pl.CostEstimate(
            flops=400_000_000, bytes_accessed=4_000_000, transcendentals=0
        ),
    )(
        coupling,
        vertical,
        jnp.swapaxes(source, 1, 2),
        jnp.swapaxes(previous, 1, 2),
        spread_rate.reshape(1, W),
    )
    return jnp.swapaxes(solved, 1, 2)


def solution(mesh):
    cells = P("gx", None, None)
    slab = P("gx", "gy", None)
    return jax.shard_map(
        local,
        mesh=mesh,
        in_specs=(cells, cells, slab, slab, P()),
        out_specs=slab,
        check_vma=False,
    )
```

```python
import jax
import jax.numpy as jnp
from jax import lax
from jax.experimental import pallas as pl
from jax.experimental.pallas import tpu as pltpu
from jax.sharding import PartitionSpec as P

CELLS = 16
ROWS = 128
W = 64
CHIPS_Z = 8
CHIPS_Y = 4
CHIPS_X = 4
MESH = pl.DeviceIdType.MESH


def dot(left, right, left_dim=1):
    return lax.dot_general(
        left,
        right,
        (((left_dim,), (0,)), ((), ())),
        precision=lax.Precision.HIGH,
        preferred_element_type=jnp.float32,
    )


def iota(shape, dim):
    return lax.broadcasted_iota(jnp.int32, shape, dim)


def lane_copy(value, lane):
    return jnp.broadcast_to(value[:, lane : lane + 1], value.shape)


def pivot_block(rows, head):
    count = len(head)
    sub = iota((count, 128), 0)
    head = list(head)
    recip = 1.0 / head[0][0:1]
    for j in range(count):
        next_recip = None
        if j < count - 1:
            cross = head[j][j + 1 : j + 2] * head[j + 1][j : j + 1]
            next_recip = 1.0 / (head[j + 1][j + 1 : j + 2] - cross * recip)
        row = rows[j : j + 1] * recip
        for k in range(j + 1, count):
            entry = head[k][j : j + 1] * recip
            head[k] = jnp.where(sub == j, entry, head[k] - head[j] * entry)
        rows = jnp.where(sub == j, row, rows - head[j] * row)
        recip = next_recip
    return rows


def sum_of(terms):
    while len(terms) > 1:
        pairs = [terms[i] + terms[i + 1] for i in range(0, len(terms) - 1, 2)]
        terms = pairs + terms[2 * len(pairs) :]
    return terms[0]


def inverses_of(matrices):
    alone = len(matrices) == 1
    size = 16 if alone else 8
    count = W // size
    blocks = [[m[size * t : size * (t + 1)] for t in range(count)] for m in matrices]
    for k in range(count):
        first = size * k
        lead = first + W if alone else first
        tops = [
            pivot_block(rows[k], [lane_copy(rows[k], lead + j) for j in range(size)])
            for rows in blocks
        ]
        others = [t for t in range(count) if t != k]
        near = others if alone else [(k + 1) % count]
        far = [t for t in others if t not in near]
        for rows, top in zip(blocks, tops):
            for t in near:
                rows[t] = rows[t] - sum_of(
                    [lane_copy(rows[t], lead + j) * top[j : j + 1] for j in range(size)]
                )
            if far:
                parts = [top]
                if first > 0:
                    parts = [jnp.zeros((first, 128), jnp.float32)] + parts
                if first + size < W:
                    parts = parts + [jnp.zeros((W - size - first, 128), jnp.float32)]
                taken = dot(
                    jnp.concatenate([rows[t] for t in far], axis=0)[:, :W],
                    jnp.concatenate(parts, axis=0),
                )
                for at, t in enumerate(far):
                    rows[t] = rows[t] - taken[size * at : size * (at + 1)]
            rows[k] = top
    return [jnp.concatenate(rows, axis=0) for rows in blocks]


def augmented(link_excess, left, alone, symmetric=False):
    lane = iota((W, 128), 1)
    eye = ((lane & (W - 1)) == iota((W, 128), 0)).astype(jnp.float32)
    value = link_excess + pltpu.roll(link_excess, W, 1)
    if left is not None:
        value = value + (left if symmetric else jnp.concatenate([left, left], axis=0).T[:W])
    return jnp.where((lane >= W) if alone else (lane < W), value, eye)


def high_lanes(value):
    return jnp.where(iota(value.shape, 1) < W, 0.0, value)


def picks_of(stride, count):
    return range(stride, count, 2 * stride)


def strides_of(count):
    return [1 << k for k in range(count.bit_length() - 1)]


def reduce_links(links, ghost, solved, inverses, count, stride, symmetric=False):
    picks = picks_of(stride, count)
    alone = len(picks) == 1
    found = inverses_of(
        [augmented(links[i], links[i - stride], alone, symmetric) for i in picks]
    )
    for at, i in enumerate(picks):
        if alone:
            inverses[i] = found[at]
            answer = dot(found[at][:, :W], links[i])
        else:
            inverses[i] = pltpu.roll(found[at], W, 1)
            answer = dot(
                found[at],
                jnp.concatenate([jnp.zeros((W, 128), jnp.float32), links[i]], axis=0),
            )
        solved[i] = answer
        before = links[i - stride]
        links[i - stride] = high_lanes(before) + dot(before[:, :W], answer)
        if i + stride < count:
            links[i + stride] = links[i + stride] + high_lanes(dot(links[i][:, :W], answer, 0))
        elif ghost is not None:
            ghost[...] = ghost[...] + high_lanes(dot(links[i][:, :W], answer, 0))


def reduce_rhs(rhs, ghost, solved, inverses, count, stride):
    for i in picks_of(stride, count):
        own = rhs[i]
        passed = dot(solved[i], own, 0)
        rhs[i - stride] = rhs[i - stride] + (own - passed[:W] - passed[W:])
        if i + stride < count:
            rhs[i + stride] = rhs[i + stride] + passed[:W]
        elif ghost is not None:
            ghost[...] = ghost[...] + passed[:W]
        rhs[i] = dot(inverses[i][:, :W], own)


def expand(solved, rhs, field, count):
    for stride in reversed(strides_of(count)):
        for i in picks_of(stride, count):
            before, after = field[i - stride], field[i + stride]
            change = jnp.concatenate([after - before, -before], axis=0)
            field[i] = rhs[i] + before + dot(solved[i], change)


def packed_links(link_excess, ghost):
    low = pltpu.roll(ghost[: W // 2], W, 1)
    return jnp.concatenate([link_excess, low + high_lanes(ghost[W // 2 :])], axis=0)


def unpacked_ghost(packed):
    tail = packed[W:]
    return high_lanes(jnp.concatenate([pltpu.roll(tail, W, 1), tail], axis=0))


def chain_links(packed, links, ghost, count):
    for i in range(count):
        value = packed(i)[:W]
        if i > 0:
            value = value + unpacked_ghost(packed(i - 1))
        links[i] = value
    if ghost is not None:
        ghost[...] = unpacked_ghost(packed(count - 1))


def chain_rhs(own, passed, rhs, ghost, count):
    for i in range(count):
        rhs[i] = own(i) + passed(i - 1) if i > 0 else own(i)
    if ghost is not None:
        ghost[...] = passed(count - 1)


def kernel(coupling, vertical, source, previous, rate, out, *scratch):
    (coupling_in, vertical_in, source_in, previous_in, in_sems) = scratch[:5]
    (edge_out, edge_in, edge_send, edge_recv) = scratch[5:9]
    (links, ghost, solved, inverses, rhs, rhs_ghost, field) = scratch[9:16]
    (p_slots, p_links, p_ghost, p_solved, p_inverses) = scratch[16:21]
    (p_rslots, p_rhs, p_rhs_ghost, p_field, p_send, p_recv) = scratch[21:27]
    (z_slots, z_links, z_ghost, z_solved, z_inverses) = scratch[27:32]
    (z_rslots, z_rhs, z_rhs_ghost, z_field, z_send, z_recv, f_send, f_recv) = scratch[32:40]
    (y_slots, y_links, y_solved, y_inverses) = scratch[40:44]
    (y_rslots, y_rhs, y_field, y_send, y_recv) = scratch[44:49]

    gx, gy = lax.axis_index("gx"), lax.axis_index("gy")
    core = lax.rem(gx, 2)
    chip = lax.div(gx, 2)
    z = lax.rem(chip, CHIPS_Z)
    y = lax.div(chip, CHIPS_Z)

    def at(y_, z_, core_):
        return (y_ * CHIPS_Z + z_) * 2 + core_

    x_up = (gx, lax.rem(gy + 1, CHIPS_X))
    x_down = (gx, lax.rem(gy + CHIPS_X - 1, CHIPS_X))
    partner = (at(y, z, 1 - core), gy)
    z_to = {d: (at(y, lax.rem(z + d, CHIPS_Z), core), gy) for d in range(1, CHIPS_Z)}
    y_to = {d: (at(lax.rem(y + d, CHIPS_Y), z, core), gy) for d in range(1, CHIPS_Y)}
    z_order = (4, 3, 5, 2, 6, 1, 7)
    z_arrive = (1, 7, 2, 6, 3, 5, 4)
    y_order = (2, 1, 3)

    barrier = pltpu.get_barrier_semaphore()
    everyone = [x_up, x_down, partner] + list(z_to.values()) + list(y_to.values())
    for peer in everyone:
        pl.semaphore_signal(barrier, inc=1, device_id=peer, device_id_type=MESH)
    loads = [
        pltpu.make_async_copy(src, dst, in_sems.at[k])
        for k, (src, dst) in enumerate(
            [
                (coupling, coupling_in),
                (vertical, vertical_in),
                (previous, previous_in),
                (source, source_in),
            ]
        )
    ]
    for load in loads:
        load.start()

    def remote(src, dst, send, recv, peer):
        copy = pltpu.make_async_remote_copy(
            src_ref=src,
            dst_ref=dst,
            send_sem=send,
            recv_sem=recv,
            device_id=peer,
            device_id_type=MESH,
        )
        copy.start()
        return copy

    lane = iota((W, 128), 1)
    loads[0].wait()
    loads[1].wait()
    for i in range(CELLS):
        links[i, :, 0:W] = coupling_in[i]
        links[i, :, W:128] = vertical_in[i]
    ghost[...] = jnp.zeros_like(ghost)
    reduce_links(links, ghost, solved, inverses, CELLS, 1, True)

    loads[2].wait()
    edges_value = jnp.zeros((W, 128), jnp.float32)
    for i in range(CELLS):
        own = previous_in[i]
        edges_value = jnp.where(lane == i, pltpu.roll(own, i + 1, 1), edges_value)
        edges_value = jnp.where(lane == W + i, pltpu.roll(own, W + i, 1), edges_value)
    edge_out[...] = edges_value
    for stride in strides_of(CELLS)[1:]:
        reduce_links(links, ghost, solved, inverses, CELLS, stride)

    pl.semaphore_wait(barrier, len(everyone))
    edges = [
        remote(edge_out, edge_in.at[0], edge_send.at[0], edge_recv.at[0], x_up),
        remote(edge_out, edge_in.at[1], edge_send.at[1], edge_recv.at[1], x_down),
    ]

    p_slots[core] = packed_links(links[0], ghost[...])
    p_copy = remote(p_slots.at[core], p_slots.at[core], p_send.at[0], p_recv.at[0], partner)

    p_copy.wait()
    chain_links(lambda i: p_slots[i], p_links, p_ghost, 2)
    reduce_links(p_links, p_ghost, p_solved, p_inverses, 2, 1)

    payload = packed_links(p_links[0], p_ghost[...])
    z_slots[0, z] = payload[:48]
    z_slots[1, z] = payload[48:]
    z_copies = {
        d: remote(
            z_slots.at[core, z],
            z_slots.at[core, z],
            z_send.at[0, d - 1],
            z_recv.at[0, d - 1],
            z_to[d],
        )
        for d in z_order
    }

    loads[3].wait()
    for edge in edges:
        edge.wait()
    speed = jnp.broadcast_to(rate[...], (128, W)).T
    for i in range(CELLS):
        own = previous_in[i]
        below = jnp.where(
            lane == 0, pltpu.roll(edge_in[0], (128 - i) % 128, 1), pltpu.roll(own, 1, 1)
        )
        above = jnp.where(
            lane == 127, pltpu.roll(edge_in[1], 127 - W - i, 1), pltpu.roll(own, 127, 1)
        )
        rhs[i] = source_in[i] + speed * (above + below - 2.0 * own)
    rhs_ghost[...] = jnp.zeros_like(rhs_ghost)

    for stride in strides_of(CELLS):
        reduce_rhs(rhs, rhs_ghost, solved, inverses, CELLS, stride)
    p_rslots[core, 0] = rhs[0]
    p_rslots[core, 1] = rhs_ghost[...]
    p_copy = remote(p_rslots.at[core], p_rslots.at[core], p_send.at[1], p_recv.at[1], partner)
    p_copy.wait()
    chain_rhs(lambda i: p_rslots[i, 0], lambda i: p_rslots[i, 1], p_rhs, p_rhs_ghost, 2)
    reduce_rhs(p_rhs, p_rhs_ghost, p_solved, p_inverses, 2, 1)
    z_rslots[0, z] = p_rhs[0]
    z_rslots[1, z] = p_rhs_ghost[...]

    def forward(slots, copies, which):
        passed = []
        for d in z_arrive:
            copies[d].wait_recv()
            behind = lax.rem(z + CHIPS_Z - d, CHIPS_Z)
            passed.append(
                remote(
                    slots.at[core, behind],
                    slots.at[core, behind],
                    f_send.at[which, d - 1],
                    f_recv.at[which, d - 1],
                    partner,
                )
            )
        return passed

    z_passed = forward(z_slots, z_copies, 0)
    zr_copies = {
        d: remote(
            z_rslots.at[core, z],
            z_rslots.at[core, z],
            z_send.at[1, d - 1],
            z_recv.at[1, d - 1],
            z_to[d],
        )
        for d in z_order
    }
    for copy in z_passed:
        copy.wait()
    chain_links(
        lambda i: jnp.concatenate([z_slots[0, i], z_slots[1, i]], axis=0),
        z_links,
        z_ghost,
        CHIPS_Z,
    )
    for stride in strides_of(CHIPS_Z):
        reduce_links(z_links, z_ghost, z_solved, z_inverses, CHIPS_Z, stride)

    y_slots[y] = packed_links(z_links[0], z_ghost[...])
    y_copies = [
        remote(y_slots.at[y], y_slots.at[y], y_send.at[0, d - 1], y_recv.at[0, d - 1], y_to[d])
        for d in y_order
    ]
    for copy in forward(z_rslots, zr_copies, 1):
        copy.wait()
    chain_rhs(lambda i: z_rslots[0, i], lambda i: z_rslots[1, i], z_rhs, z_rhs_ghost, CHIPS_Z)
    for stride in strides_of(CHIPS_Z):
        reduce_rhs(z_rhs, z_rhs_ghost, z_solved, z_inverses, CHIPS_Z, stride)
    y_rslots[y, 0] = z_rhs[0]
    y_rslots[y, 1] = z_rhs_ghost[...]
    yr_copies = [
        remote(
            y_rslots.at[y], y_rslots.at[y], y_send.at[1, d - 1], y_recv.at[1, d - 1], y_to[d]
        )
        for d in y_order
    ]
    for copy in y_copies:
        copy.wait()
    chain_links(lambda i: y_slots[i], y_links, None, CHIPS_Y)
    for stride in strides_of(CHIPS_Y):
        reduce_links(y_links, None, y_solved, y_inverses, CHIPS_Y, stride)
    first = inverses_of([augmented(y_links[0], None, True)])

    for copy in yr_copies:
        copy.wait()
    chain_rhs(lambda i: y_rslots[i, 0], lambda i: y_rslots[i, 1], y_rhs, None, CHIPS_Y)
    for stride in strides_of(CHIPS_Y):
        reduce_rhs(y_rhs, None, y_solved, y_inverses, CHIPS_Y, stride)
    y_field[0] = dot(first[0][:, :W], y_rhs[0])
    y_field[CHIPS_Y] = jnp.zeros((W, ROWS), jnp.float32)
    expand(y_solved, y_rhs, y_field, CHIPS_Y)
    z_field[0] = y_field[y]
    z_field[CHIPS_Z] = y_field[y + 1]
    expand(z_solved, z_rhs, z_field, CHIPS_Z)
    p_field[0] = z_field[z]
    p_field[2] = z_field[z + 1]
    expand(p_solved, p_rhs, p_field, 2)
    field[0] = p_field[core]
    field[CELLS] = p_field[core + 1]
    expand(solved, rhs, field, CELLS)
    for i in range(CELLS):
        out[i] = field[i]
    for d in z_order:
        z_copies[d].wait_send()
        zr_copies[d].wait_send()


def local(coupling, vertical, source, previous, spread_rate):
    f32 = jnp.float32

    def vmem(*shape):
        return pltpu.VMEM(shape + (128,), f32)

    dma = pltpu.SemaphoreType.DMA

    def level(count):
        return [vmem(count, W), vmem(W), vmem(count, W), vmem(count, W)]

    def level_rhs(count):
        return [vmem(count, W), vmem(W), vmem(count + 1, W)]

    scratch = [
        pltpu.VMEM((CELLS, W, W), f32),
        pltpu.VMEM((CELLS, W, W), f32),
        vmem(CELLS, W),
        vmem(CELLS, W),
        dma((4,)),
        vmem(W),
        vmem(2, W),
        dma((2,)),
        dma((2,)),
    ]
    scratch += level(CELLS) + level_rhs(CELLS)
    scratch += [vmem(2, 96)] + level(2)
    scratch += [vmem(2, 2, W)] + level_rhs(2) + [dma((2,)), dma((2,))]
    scratch += [vmem(2, CHIPS_Z, 48)] + level(CHIPS_Z)
    scratch += [vmem(2, CHIPS_Z, W)] + level_rhs(CHIPS_Z) + [dma((2, CHIPS_Z - 1))] * 4
    scratch += [vmem(CHIPS_Y, 96), vmem(CHIPS_Y, W), vmem(CHIPS_Y, W), vmem(CHIPS_Y, W)]
    scratch += [vmem(CHIPS_Y, 2, W), vmem(CHIPS_Y, W), vmem(CHIPS_Y + 1, W)]
    scratch += [dma((2, CHIPS_Y - 1))] * 2
    anywhere = pl.BlockSpec(memory_space=pl.ANY)
    solved = pl.pallas_call(
        kernel,
        out_shape=jax.ShapeDtypeStruct((CELLS, W, ROWS), f32),
        in_specs=[anywhere] * 4 + [pl.BlockSpec(memory_space=pltpu.VMEM)],
        out_specs=pl.BlockSpec(memory_space=pltpu.VMEM),
        scratch_shapes=scratch,
        compiler_params=pltpu.CompilerParams(
            collective_id=0, has_side_effects=True, vmem_limit_bytes=60 * 1024 * 1024
        ),
        cost_estimate=pl.CostEstimate(
            flops=400_000_000, bytes_accessed=4_000_000, transcendentals=0
        ),
    )(
        coupling,
        vertical,
        jnp.swapaxes(source, 1, 2),
        jnp.swapaxes(previous, 1, 2),
        spread_rate.reshape(1, W),
    )
    return jnp.swapaxes(solved, 1, 2)


def solution(mesh):
    cells = P("gx", None, None)
    slab = P("gx", "gy", None)
    return jax.shard_map(
        local,
        mesh=mesh,
        in_specs=(cells, cells, slab, slab, P()),
        out_specs=slab,
        check_vma=False,
    )
```

```python
import jax
import jax.numpy as jnp
from jax import lax
from jax.experimental import pallas as pl
from jax.experimental.pallas import tpu as pltpu
from jax.sharding import PartitionSpec as P

CELLS = 16
ROWS = 128
W = 64
CHIPS_Z = 8
CHIPS_Y = 4
CHIPS_X = 4
MESH = pl.DeviceIdType.MESH


def dot(left, right, left_dim=1):
    return lax.dot_general(
        left,
        right,
        (((left_dim,), (0,)), ((), ())),
        precision=lax.Precision.HIGH,
        preferred_element_type=jnp.float32,
    )


def iota(shape, dim):
    return lax.broadcasted_iota(jnp.int32, shape, dim)


def lane_copy(value, lane):
    return jnp.broadcast_to(value[:, lane : lane + 1], value.shape)


def pivot_block(rows, head):
    count = len(head)
    sub = iota((count, 128), 0)
    head = list(head)
    recip = 1.0 / head[0][0:1]
    for j in range(count):
        next_recip = None
        if j < count - 1:
            cross = head[j][j + 1 : j + 2] * head[j + 1][j : j + 1]
            next_recip = 1.0 / (head[j + 1][j + 1 : j + 2] - cross * recip)
        row = rows[j : j + 1] * recip
        for k in range(j + 1, count):
            entry = head[k][j : j + 1] * recip
            head[k] = jnp.where(sub == j, entry, head[k] - head[j] * entry)
        rows = jnp.where(sub == j, row, rows - head[j] * row)
        recip = next_recip
    return rows


def sum_of(terms):
    while len(terms) > 1:
        pairs = [terms[i] + terms[i + 1] for i in range(0, len(terms) - 1, 2)]
        terms = pairs + terms[2 * len(pairs) :]
    return terms[0]


def inverses_of(matrices):
    alone = len(matrices) == 1
    size = 16 if alone else 8
    count = W // size
    blocks = [[m[size * t : size * (t + 1)] for t in range(count)] for m in matrices]
    for k in range(count):
        first = size * k
        lead = first + W if alone else first
        tops = [
            pivot_block(rows[k], [lane_copy(rows[k], lead + j) for j in range(size)])
            for rows in blocks
        ]
        others = [t for t in range(count) if t != k]
        near = others if alone else [(k + 1) % count]
        far = [t for t in others if t not in near]
        for rows, top in zip(blocks, tops):
            for t in near:
                rows[t] = rows[t] - sum_of(
                    [lane_copy(rows[t], lead + j) * top[j : j + 1] for j in range(size)]
                )
            if far:
                parts = [top]
                if first > 0:
                    parts = [jnp.zeros((first, 128), jnp.float32)] + parts
                if first + size < W:
                    parts = parts + [jnp.zeros((W - size - first, 128), jnp.float32)]
                taken = dot(
                    jnp.concatenate([rows[t] for t in far], axis=0)[:, :W],
                    jnp.concatenate(parts, axis=0),
                )
                for at, t in enumerate(far):
                    rows[t] = rows[t] - taken[size * at : size * (at + 1)]
            rows[k] = top
    return [jnp.concatenate(rows, axis=0) for rows in blocks]


def augmented(link_excess, left, alone, symmetric=False):
    lane = iota((W, 128), 1)
    eye = ((lane & (W - 1)) == iota((W, 128), 0)).astype(jnp.float32)
    value = link_excess + pltpu.roll(link_excess, W, 1)
    if left is not None:
        value = value + (left if symmetric else jnp.concatenate([left, left], axis=0).T[:W])
    return jnp.where((lane >= W) if alone else (lane < W), value, eye)


def high_lanes(value):
    return jnp.where(iota(value.shape, 1) < W, 0.0, value)


def picks_of(stride, count):
    return range(stride, count, 2 * stride)


def strides_of(count):
    return [1 << k for k in range(count.bit_length() - 1)]


def reduce_links(links, ghost, solved, inverses, count, stride, symmetric=False):
    picks = picks_of(stride, count)
    alone = len(picks) == 1
    found = inverses_of(
        [augmented(links[i], links[i - stride], alone, symmetric) for i in picks]
    )
    for at, i in enumerate(picks):
        if alone:
            inverses[i] = found[at]
            answer = dot(found[at][:, :W], links[i])
        else:
            inverses[i] = pltpu.roll(found[at], W, 1)
            answer = dot(
                found[at],
                jnp.concatenate([jnp.zeros((W, 128), jnp.float32), links[i]], axis=0),
            )
        solved[i] = answer
        before = links[i - stride]
        links[i - stride] = high_lanes(before) + dot(before[:, :W], answer)
        if i + stride < count:
            links[i + stride] = links[i + stride] + high_lanes(dot(links[i][:, :W], answer, 0))
        elif ghost is not None:
            ghost[...] = ghost[...] + high_lanes(dot(links[i][:, :W], answer, 0))


def reduce_rhs(rhs, ghost, solved, inverses, count, stride):
    for i in picks_of(stride, count):
        own = rhs[i]
        passed = dot(solved[i], own, 0)
        rhs[i - stride] = rhs[i - stride] + (own - passed[:W] - passed[W:])
        if i + stride < count:
            rhs[i + stride] = rhs[i + stride] + passed[:W]
        elif ghost is not None:
            ghost[...] = ghost[...] + passed[:W]
        rhs[i] = dot(inverses[i][:, :W], own)


def expand(solved, rhs, field, count):
    for stride in reversed(strides_of(count)):
        for i in picks_of(stride, count):
            before, after = field[i - stride], field[i + stride]
            change = jnp.concatenate([after - before, -before], axis=0)
            field[i] = rhs[i] + before + dot(solved[i], change)


def expand_maps(solved, rhs, maps, count):
    for stride in reversed(strides_of(count)):
        for i in picks_of(stride, count):
            before = jnp.concatenate([maps[i - stride, 0], maps[i - stride, 1]], axis=1)
            after = jnp.concatenate([maps[i + stride, 0], maps[i + stride, 1]], axis=1)
            change = jnp.concatenate([after - before, -before], axis=0)
            found = before + dot(solved[i], change)
            maps[i, 0] = found[:, :128]
            maps[i, 1] = found[:, 128:] + rhs[i]


def packed_links(link_excess, ghost):
    low = pltpu.roll(ghost[: W // 2], W, 1)
    return jnp.concatenate([link_excess, low + high_lanes(ghost[W // 2 :])], axis=0)


def unpacked_ghost(packed):
    tail = packed[W:]
    return high_lanes(jnp.concatenate([pltpu.roll(tail, W, 1), tail], axis=0))


def chain_links(packed, links, ghost, count):
    for i in range(count):
        value = packed(i)[:W]
        if i > 0:
            value = value + unpacked_ghost(packed(i - 1))
        links[i] = value
    if ghost is not None:
        ghost[...] = unpacked_ghost(packed(count - 1))


def chain_rhs(own, passed, rhs, ghost, count):
    for i in range(count):
        rhs[i] = own(i) + passed(i - 1) if i > 0 else own(i)
    if ghost is not None:
        ghost[...] = passed(count - 1)


def kernel(coupling, vertical, source, previous, rate, out, *scratch):
    (coupling_in, vertical_in, source_in, previous_in, in_sems) = scratch[:5]
    (edge_out, edge_in, edge_send, edge_recv) = scratch[5:9]
    (links, ghost, solved, inverses, rhs, rhs_ghost, field) = scratch[9:16]
    (p_slots, p_links, p_ghost, p_solved, p_inverses) = scratch[16:21]
    (p_rslots, p_rhs, p_rhs_ghost, p_maps, p_send, p_recv) = scratch[21:27]
    (z_slots, z_links, z_ghost, z_solved, z_inverses) = scratch[27:32]
    (z_rslots, z_rhs, z_rhs_ghost, z_maps, z_send, z_recv, f_send, f_recv) = scratch[32:40]
    (y_slots, y_links, y_solved, y_inverses) = scratch[40:44]
    (y_rslots, y_rhs, y_field, y_send, y_recv) = scratch[44:49]

    gx, gy = lax.axis_index("gx"), lax.axis_index("gy")
    core = lax.rem(gx, 2)
    chip = lax.div(gx, 2)
    z = lax.rem(chip, CHIPS_Z)
    y = lax.div(chip, CHIPS_Z)

    def at(y_, z_, core_):
        return (y_ * CHIPS_Z + z_) * 2 + core_

    x_up = (gx, lax.rem(gy + 1, CHIPS_X))
    x_down = (gx, lax.rem(gy + CHIPS_X - 1, CHIPS_X))
    partner = (at(y, z, 1 - core), gy)
    z_to = {d: (at(y, lax.rem(z + d, CHIPS_Z), core), gy) for d in range(1, CHIPS_Z)}
    y_to = {d: (at(lax.rem(y + d, CHIPS_Y), z, core), gy) for d in range(1, CHIPS_Y)}
    z_order = (4, 3, 5, 2, 6, 1, 7)
    z_arrive = (1, 7, 2, 6, 3, 5, 4)
    y_order = (2, 1, 3)

    barrier = pltpu.get_barrier_semaphore()
    everyone = [x_up, x_down, partner] + list(z_to.values()) + list(y_to.values())
    for peer in everyone:
        pl.semaphore_signal(barrier, inc=1, device_id=peer, device_id_type=MESH)
    loads = [
        pltpu.make_async_copy(src, dst, in_sems.at[k])
        for k, (src, dst) in enumerate(
            [
                (coupling, coupling_in),
                (vertical, vertical_in),
                (previous, previous_in),
                (source, source_in),
            ]
        )
    ]
    for load in loads:
        load.start()

    def remote(src, dst, send, recv, peer):
        copy = pltpu.make_async_remote_copy(
            src_ref=src,
            dst_ref=dst,
            send_sem=send,
            recv_sem=recv,
            device_id=peer,
            device_id_type=MESH,
        )
        copy.start()
        return copy

    lane = iota((W, 128), 1)
    loads[0].wait()
    loads[1].wait()
    for i in range(CELLS):
        links[i, :, 0:W] = coupling_in[i]
        links[i, :, W:128] = vertical_in[i]
    ghost[...] = jnp.zeros_like(ghost)
    reduce_links(links, ghost, solved, inverses, CELLS, 1, True)

    for stride in strides_of(CELLS)[1:]:
        reduce_links(links, ghost, solved, inverses, CELLS, stride)

    pl.semaphore_wait(barrier, len(everyone))
    p_slots[core] = packed_links(links[0], ghost[...])
    p_copy = remote(p_slots.at[core], p_slots.at[core], p_send.at[0], p_recv.at[0], partner)

    loads[2].wait()
    edges_value = jnp.zeros((W, 128), jnp.float32)
    for i in range(CELLS):
        own = previous_in[i]
        edges_value = jnp.where(lane == i, pltpu.roll(own, i + 1, 1), edges_value)
        edges_value = jnp.where(lane == W + i, pltpu.roll(own, W + i, 1), edges_value)
    edge_out[...] = edges_value
    edges = [
        remote(edge_out, edge_in.at[0], edge_send.at[0], edge_recv.at[0], x_up),
        remote(edge_out, edge_in.at[1], edge_send.at[1], edge_recv.at[1], x_down),
    ]

    p_copy.wait()
    chain_links(lambda i: p_slots[i], p_links, p_ghost, 2)
    reduce_links(p_links, p_ghost, p_solved, p_inverses, 2, 1)

    payload = packed_links(p_links[0], p_ghost[...])
    z_slots[0, z] = payload[:48]
    z_slots[1, z] = payload[48:]
    z_copies = {
        d: remote(
            z_slots.at[core, z],
            z_slots.at[core, z],
            z_send.at[0, d - 1],
            z_recv.at[0, d - 1],
            z_to[d],
        )
        for d in z_order
    }

    loads[3].wait()
    for edge in edges:
        edge.wait()
    speed = jnp.broadcast_to(rate[...], (128, W)).T
    for i in range(CELLS):
        own = previous_in[i]
        below = jnp.where(
            lane == 0, pltpu.roll(edge_in[0], (128 - i) % 128, 1), pltpu.roll(own, 1, 1)
        )
        above = jnp.where(
            lane == 127, pltpu.roll(edge_in[1], 127 - W - i, 1), pltpu.roll(own, 127, 1)
        )
        rhs[i] = source_in[i] + speed * (above + below - 2.0 * own)
    rhs_ghost[...] = jnp.zeros_like(rhs_ghost)

    for stride in strides_of(CELLS):
        reduce_rhs(rhs, rhs_ghost, solved, inverses, CELLS, stride)
    p_rslots[core, 0] = rhs[0]
    p_rslots[core, 1] = rhs_ghost[...]
    p_copy = remote(p_rslots.at[core], p_rslots.at[core], p_send.at[1], p_recv.at[1], partner)
    p_copy.wait()
    chain_rhs(lambda i: p_rslots[i, 0], lambda i: p_rslots[i, 1], p_rhs, p_rhs_ghost, 2)
    reduce_rhs(p_rhs, p_rhs_ghost, p_solved, p_inverses, 2, 1)
    z_rslots[0, z] = p_rhs[0]
    z_rslots[1, z] = p_rhs_ghost[...]

    def forward(slots, copies, which):
        passed = []
        for d in z_arrive:
            copies[d].wait_recv()
            behind = lax.rem(z + CHIPS_Z - d, CHIPS_Z)
            passed.append(
                remote(
                    slots.at[core, behind],
                    slots.at[core, behind],
                    f_send.at[which, d - 1],
                    f_recv.at[which, d - 1],
                    partner,
                )
            )
        return passed

    z_passed = forward(z_slots, z_copies, 0)
    zr_copies = {
        d: remote(
            z_rslots.at[core, z],
            z_rslots.at[core, z],
            z_send.at[1, d - 1],
            z_recv.at[1, d - 1],
            z_to[d],
        )
        for d in z_order
    }
    for copy in z_passed:
        copy.wait()
    chain_links(
        lambda i: jnp.concatenate([z_slots[0, i], z_slots[1, i]], axis=0),
        z_links,
        z_ghost,
        CHIPS_Z,
    )
    for stride in strides_of(CHIPS_Z):
        reduce_links(z_links, z_ghost, z_solved, z_inverses, CHIPS_Z, stride)

    y_slots[y] = packed_links(z_links[0], z_ghost[...])
    y_copies = [
        remote(y_slots.at[y], y_slots.at[y], y_send.at[0, d - 1], y_recv.at[0, d - 1], y_to[d])
        for d in y_order
    ]
    for copy in forward(z_rslots, zr_copies, 1):
        copy.wait()
    chain_rhs(lambda i: z_rslots[0, i], lambda i: z_rslots[1, i], z_rhs, z_rhs_ghost, CHIPS_Z)
    for stride in strides_of(CHIPS_Z):
        reduce_rhs(z_rhs, z_rhs_ghost, z_solved, z_inverses, CHIPS_Z, stride)
    y_rslots[y, 0] = z_rhs[0]
    y_rslots[y, 1] = z_rhs_ghost[...]
    yr_copies = [
        remote(
            y_rslots.at[y], y_rslots.at[y], y_send.at[1, d - 1], y_recv.at[1, d - 1], y_to[d]
        )
        for d in y_order
    ]
    spot = (lane & (W - 1)) == iota((W, 128), 0)
    z_maps[0, 0] = jnp.where(spot & (lane >= W), -1.0, 0.0)
    z_maps[CHIPS_Z, 0] = jnp.where(spot, jnp.where(lane >= W, -1.0, 1.0), 0.0)
    z_maps[0, 1] = jnp.zeros((W, ROWS), jnp.float32)
    z_maps[CHIPS_Z, 1] = jnp.zeros((W, ROWS), jnp.float32)
    expand_maps(z_solved, z_rhs, z_maps, CHIPS_Z)
    p_maps[0] = z_maps[z]
    p_maps[2] = z_maps[z + 1]
    expand_maps(p_solved, p_rhs, p_maps, 2)

    for copy in y_copies:
        copy.wait()
    chain_links(lambda i: y_slots[i], y_links, None, CHIPS_Y)
    for stride in strides_of(CHIPS_Y):
        reduce_links(y_links, None, y_solved, y_inverses, CHIPS_Y, stride)
    for copy in yr_copies:
        copy.wait()
    chain_rhs(lambda i: y_rslots[i, 0], lambda i: y_rslots[i, 1], y_rhs, None, CHIPS_Y)
    for stride in strides_of(CHIPS_Y):
        reduce_rhs(y_rhs, None, y_solved, y_inverses, CHIPS_Y, stride)
    first = inverses_of([augmented(y_links[0], None, True)])
    y_field[0] = dot(first[0][:, :W], y_rhs[0])
    y_field[CHIPS_Y] = jnp.zeros((W, ROWS), jnp.float32)
    expand(y_solved, y_rhs, y_field, CHIPS_Y)
    change = jnp.concatenate([y_field[y + 1] - y_field[y], -y_field[y]], axis=0)
    ends = dot(jnp.concatenate([p_maps[core, 0], p_maps[core + 1, 0]], axis=0), change)
    field[0] = ends[:W] + p_maps[core, 1]
    field[CELLS] = ends[W:] + p_maps[core + 1, 1]
    expand(solved, rhs, field, CELLS)
    for i in range(CELLS):
        out[i] = field[i]
    for d in z_order:
        z_copies[d].wait_send()
        zr_copies[d].wait_send()


def local(coupling, vertical, source, previous, spread_rate):
    f32 = jnp.float32

    def vmem(*shape):
        return pltpu.VMEM(shape + (128,), f32)

    dma = pltpu.SemaphoreType.DMA

    def level(count):
        return [vmem(count, W), vmem(W), vmem(count, W), vmem(count, W)]

    def level_rhs(count, *parts):
        return [vmem(count, W), vmem(W), vmem(count + 1, *parts, W)]

    scratch = [
        pltpu.VMEM((CELLS, W, W), f32),
        pltpu.VMEM((CELLS, W, W), f32),
        vmem(CELLS, W),
        vmem(CELLS, W),
        dma((4,)),
        vmem(W),
        vmem(2, W),
        dma((2,)),
        dma((2,)),
    ]
    scratch += level(CELLS) + level_rhs(CELLS)
    scratch += [vmem(2, 96)] + level(2)
    scratch += [vmem(2, 2, W)] + level_rhs(2, 2) + [dma((2,)), dma((2,))]
    scratch += [vmem(2, CHIPS_Z, 48)] + level(CHIPS_Z)
    scratch += [vmem(2, CHIPS_Z, W)] + level_rhs(CHIPS_Z, 2) + [dma((2, CHIPS_Z - 1))] * 4
    scratch += [vmem(CHIPS_Y, 96), vmem(CHIPS_Y, W), vmem(CHIPS_Y, W), vmem(CHIPS_Y, W)]
    scratch += [vmem(CHIPS_Y, 2, W), vmem(CHIPS_Y, W), vmem(CHIPS_Y + 1, W)]
    scratch += [dma((2, CHIPS_Y - 1))] * 2
    anywhere = pl.BlockSpec(memory_space=pl.ANY)
    solved = pl.pallas_call(
        kernel,
        out_shape=jax.ShapeDtypeStruct((CELLS, W, ROWS), f32),
        in_specs=[anywhere] * 4 + [pl.BlockSpec(memory_space=pltpu.VMEM)],
        out_specs=pl.BlockSpec(memory_space=pltpu.VMEM),
        scratch_shapes=scratch,
        compiler_params=pltpu.CompilerParams(
            collective_id=0, has_side_effects=True, vmem_limit_bytes=60 * 1024 * 1024
        ),
        cost_estimate=pl.CostEstimate(
            flops=400_000_000, bytes_accessed=4_000_000, transcendentals=0
        ),
    )(
        coupling,
        vertical,
        jnp.swapaxes(source, 1, 2),
        jnp.swapaxes(previous, 1, 2),
        spread_rate.reshape(1, W),
    )
    return jnp.swapaxes(solved, 1, 2)


def solution(mesh):
    cells = P("gx", None, None)
    slab = P("gx", "gy", None)
    return jax.shard_map(
        local,
        mesh=mesh,
        in_specs=(cells, cells, slab, slab, P()),
        out_specs=slab,
        check_vma=False,
    )
```
